32 devices in a mesh: dp: 4 (over z), expert: 8 (over y, x, core).
Axes of the slice: x: 2, y: 2, z: 4, core: 2. Of those that a mesh axis runs over, the one named last changes fastest.
Arguments:
- residual_in: bfloat16 [4096, 2048], P(('dp', 'expert')), may hold values from -40 to 40
- attention_gain: float32 [2048], replicated, may hold values from 0.25 to 1.75
- query_weight: bfloat16 [2048, 2048], P(None, 'expert'), may hold values from -0.125 to 0.125
- key_weight: bfloat16 [2048, 2048], P(None, 'expert'), may hold values from -0.125 to 0.125
- value_weight: bfloat16 [2048, 2048], P(None, 'expert'), may hold values from -0.125 to 0.125
- output_weight: bfloat16 [2048, 2048], P('expert'), may hold values from -0.125 to 0.125
- prompt_keys: bfloat16 [12, 2048, 2048], P('dp', None, 'expert'), may hold values from -220 to 220
- prompt_values: bfloat16 [12, 2048, 2048], P('dp', None, 'expert'), may hold values from -12 to 12
- group_index: int32 [4, 32], P('dp'), may hold values from 0 to 2, never falling along the last dimension, each value on 1 to 16 neighbouring positions
- prompt_length: int32 [12], P('dp'), may hold values from 1 to 2048, 12288 in all
- own_length: int32 [128], P('dp'), may hold values from 1 to 32
- expert_gain: float32 [2048], replicated, may hold values from 0.25 to 1.75
- expert_ids: int32 [4096, 8], P(('dp', 'expert')), may hold values from 0 to 31, all different within a row; in each aligned block of 128 rows (0 to 127, 128 to 255, ...) at most 48 rows name the same one
- expert_mix: float32 [4096, 8], P(('dp', 'expert')), may hold values from 0.02 to 0.3
- gate_weight: bfloat16 [32, 2048, 1024], P(('dp', 'expert')), may hold values from -0.125 to 0.125
- up_weight: bfloat16 [32, 2048, 1024], P(('dp', 'expert')), may hold values from -0.125 to 0.125
- down_weight: bfloat16 [32, 1024, 2048], P(('dp', 'expert')), may hold values from -0.1875 to 0.1875
Outputs:
- attention_update: bfloat16 [4096, 2048], P(('dp', 'expert'))
- expert_update: bfloat16 [4096, 2048], P(('dp', 'expert'))
The draws below stay inside these ranges and needn't reach their ends.
Inputs may be any that keep to these rules, and one draw needn't show every extreme that they name: `group_index`: each row holds the 32 requests of one index of dp; a group's requests are consecutive, every group has 1 to 16 requests and some group exactly 16. `prompt_length`: some prompt is exactly 2048 long. `expert_ids`: a token's 8 experts differ; among the 128 rows of one device no expert is named more than 48 times, a bound that some block reaches.
All inputs are finite; a program needn't handle non-finite values. No bound on the sum of `prompt_length` on one device may be relied on, other than what follows from the above.
Results may differ from the reference program's by a relative error of at most 0.025.
The reference program's roundings to bfloat16 on the way (of `normed`, `queries`, `weights`, `attended`, `expert_input`, `hidden` and `part`) count: a program that leaves them out, or rounds other values in their place, can miss the bound.
Values may be sent and summed in bfloat16 or wider, within the bound.
A program may use at most 128 MiB of HBM per device.

```python
import math
import jax
import jax.numpy as jnp
import numpy as np
from jax import lax

D = 2048
H = 16
HD = 128
FF = 1024
TOP = 8
EXPERTS = 32
HSPLIT = 1
FF_DEV = 1024
SHARDS = 32
REQ_DEV = 32
G_DEV = 3
GSIZE = 16
SB = 32
PMAX = 2048
REQUESTS = 128
GROUPS = 12
TOKENS = 4096
TOK_DEV = 128
CAP = 48
N_DP = 4
N_EXPERT = 8


def draw_residual_in(key, part):
    first, second = jax.random.split(key, 2)
    columns = jnp.exp(jax.random.uniform(second, (1, D), jnp.float32, math.log(0.5), math.log(5.0)))
    values = jnp.clip(jax.random.normal(first, (TOKENS, D), jnp.float32), -4.0, 4.0) * columns
    return values.astype(jnp.bfloat16)


def draw_prompt_keys(key, part):
    first = jax.random.fold_in(key, 0)
    values = jnp.clip(jax.random.normal(first, (GROUPS, PMAX, H * HD), jnp.float32), -4.0, 4.0)
    return values.astype(jnp.bfloat16)


def place_ends(values, rng, smallest, top_value):
    longest = values.shape.index(max(values.shape))
    spots = []
    for shift in (0, 1):
        where = [jax.random.randint(jax.random.fold_in(rng, axis), (), 0, length) for axis, length in enumerate(values.shape)]
        where[longest] = (where[longest] + shift) % values.shape[longest]
        spots.append(tuple(where))
    return values.at[spots[0]].set(smallest).at[spots[1]].set(top_value)


def shard_levels(rng, dims, pieces, smallest, high):
    loudness = 1.0
    for position, shards_of in pieces:
        steps = jax.random.uniform(jax.random.fold_in(jax.random.fold_in(rng, 6), position), (shards_of,), jnp.float32, smallest / len(pieces), high / len(pieces))
        loudness = loudness * jnp.repeat(jnp.exp(steps), dims[position] // shards_of).reshape((-1,) + (1,) * (len(dims) - 1 - position))
    return loudness


def split_up(number_of, total, most, slope):
    portions = [(1 << 20) // math.isqrt(rank ** slope) + 1 for rank in range(2, number_of + 1)]
    spare, given = total - most - (number_of - 1), [1] * (number_of - 1)
    while spare > 0:
        candidates = [i for i in range(number_of - 1) if given[i] < most]
        whole, left = sum([portions[i] for i in candidates]), spare
        for i in candidates:
            more = min(most - given[i], max(1, left * portions[i] // whole), spare)
            given[i] = given[i] + more
            spare = spare - more
    return np.array([most] + given)


def uneven(rng, number_of, total, most, slope):
    if number_of == 2:
        one = jax.random.randint(rng, (), max(1, total - most), min(most, total - 1) + 1)
        return jnp.stack([one, total - one])
    tallies = jnp.asarray(split_up(number_of, total, most, slope), jnp.int32)
    twos = (number_of - 1) // 2
    giver, receiver = tallies[1:1 + 2 * twos:2], tallies[2:2 + 2 * twos:2]
    room = jnp.minimum(giver - 1, most - receiver)
    shifted = jax.random.randint(jax.random.fold_in(rng, 1), (twos,), 0, 1 << 20) % (room + 1)
    tallies = tallies.at[1:1 + 2 * twos:2].set(giver - shifted).at[2:2 + 2 * twos:2].set(receiver + shifted)
    return tallies[jax.random.permutation(jax.random.fold_in(rng, 2), number_of)]


def assign_block(rng, own, number, rows, amount, top, reach, lean):
    ranking = jax.random.permutation(rng, amount)
    packed, usual = portions_of(amount, rows * top, reach, lean, True), portions_of(amount, rows * top, reach, lean, False)
    places = jnp.arange(amount)

    def named(tallies, offset_by):
        used = int((tallies > 0).sum())
        fixed = max(1, used // 4)
        passed = fixed + (places - fixed + offset_by * (used - fixed)) % max(1, amount - fixed)
        return jnp.zeros((amount,), jnp.int32).at[ranking[jnp.where(places < fixed, places, passed)]].set(jnp.asarray(tallies, jnp.int32))

    tallies = jnp.where(number % 4 == 0, named(packed, number // 4), named(usual, number - number // 4 - 1))
    mixed = jax.random.permutation(jax.random.fold_in(own, 3), amount)
    donor, receiver = mixed[0:amount // 2 * 2:2], mixed[1:amount // 2 * 2:2]
    slack = jnp.minimum(tallies[donor] - 1, reach - tallies[receiver]) // 2
    slack = jnp.where((donor == ranking[0]) | (receiver == ranking[0]) | (tallies[receiver] == 0), 0, jnp.maximum(slack, 0))
    passed = jax.random.randint(jax.random.fold_in(own, 4), (amount // 2,), 0, 1 << 20) % (slack + 1)
    tallies = tallies.at[donor].add(-passed).at[receiver].add(passed)
    labels = jnp.searchsorted(jnp.cumsum(tallies), jnp.arange(rows * top), side="right").astype(jnp.int32)
    listing = labels.reshape(top, rows).T
    listing = listing[jax.random.permutation(jax.random.fold_in(own, 1), rows)]
    offset_by = jax.random.randint(jax.random.fold_in(own, 2), (rows, 1), 0, top)
    return jnp.take_along_axis(listing, (jnp.arange(top)[None, :] + offset_by) % top, axis=1)


def portions_of(amount, total, bound, skew, full):
    weights = [(1 << 20) // math.isqrt(rank ** skew) + 1 for rank in range(1, amount + 1)]
    largest = bound if full else min(bound, max(-(-total // amount), total * weights[0] // sum(weights)))
    least = 1 if total - largest >= amount - 1 else 0
    holding, spare = [largest] + [least] * (amount - 1), total - largest - least * (amount - 1)
    while spare > 0:
        movable = [i for i in range(1, amount) if holding[i] < largest] or [i for i in range(1, amount) if holding[i] < bound]
        pool, left = sum([weights[i] for i in movable]), spare
        for i in movable:
            addition = min(bound - holding[i], max(1, left * weights[i] // pool), spare)
            holding[i] = holding[i] + addition
            spare = spare - addition
    return np.array(holding)


def bell_draw(own_key, extent, scale, most, cuts=(), kind=jnp.bfloat16):
    drawn = scale * jax.random.normal(own_key, extent, jnp.float32)
    if cuts:
        drawn = drawn * shard_levels(own_key, extent, cuts, -0.22, 0.18)
    return jnp.clip(drawn, -most, most).astype(kind)


def setup_inputs(seed: int = 0) -> dict:
    splits = jax.random.split(jax.random.key(seed), 18)
    residual_in = draw_residual_in(jax.random.fold_in(splits[17], 71), 0)
    attention_gain = jnp.clip(1.0 + 0.15 * jax.random.normal(splits[1], (D,), jnp.float32), 0.25, 1.75)
    query_weight = bell_draw(splits[2], (D, H * HD), D ** -0.5, 0.125, ((1, 8),))
    key_weight = bell_draw(splits[3], (D, H * HD), D ** -0.5, 0.125, ((1, 8),))
    value_weight = bell_draw(splits[4], (D, H * HD), D ** -0.5, 0.125, ((1, 8),))
    output_weight = bell_draw(splits[5], (H * HD, D), (H * HD) ** -0.5, 0.125, ((0, 8),))
    prompt_keys = draw_prompt_keys(jax.random.fold_in(splits[17], 71), 0)
    prompt_values = bell_draw(splits[7], (GROUPS, PMAX, H * HD), 2.0, 12.0, ((0, 4), (2, 8)))
    group_index = jax.vmap(lambda own: jnp.searchsorted(jnp.cumsum(uneven(own, G_DEV, REQ_DEV, GSIZE, 1)), jnp.arange(REQ_DEV), side="right"))(jax.random.split(splits[8], N_DP)).reshape((N_DP, REQ_DEV)).astype(jnp.int32)
    prompt_length = uneven(splits[9], GROUPS, GROUPS * PMAX // 2, PMAX, 1).astype(jnp.int32)
    own_length = place_ends(jax.random.randint(splits[10], (REQUESTS,), 1, SB + 1), jax.random.fold_in(splits[10], 1), 1, SB).astype(jnp.int32)
    expert_gain = jnp.clip(1.0 + 0.15 * jax.random.normal(splits[11], (D,), jnp.float32), 0.25, 1.75)
    expert_ids_keys = jax.random.split(jax.random.fold_in(splits[12], 1), TOKENS // TOK_DEV)
    expert_ids_turns = jax.random.permutation(jax.random.fold_in(splits[12], 3), TOKENS // TOK_DEV)
    expert_ids = jax.vmap(lambda own, number: assign_block(jax.random.fold_in(splits[12], 2), own, number, TOK_DEV, EXPERTS, TOP, CAP, 2))(expert_ids_keys, expert_ids_turns).reshape((TOKENS, TOP))
    expert_mix = jnp.clip(0.02 + 0.28 * jax.random.uniform(splits[13], (TOKENS, TOP), jnp.float32) ** shard_levels(splits[13], (TOKENS, TOP), ((0, 32),), -0.2, 0.2), 0.02, 0.3)
    gate_weight = bell_draw(splits[14], (SHARDS, D, FF_DEV), D ** -0.5, 0.125, ((0, 32),))
    up_weight = bell_draw(splits[15], (SHARDS, D, FF_DEV), D ** -0.5, 0.125, ((0, 32),))
    down_weight = bell_draw(splits[16], (SHARDS, FF_DEV, D), FF ** -0.5, 0.1875, ((0, 32),))
    return {"residual_in": residual_in, "attention_gain": attention_gain, "query_weight": query_weight, "key_weight": key_weight, "value_weight": value_weight, "output_weight": output_weight, "prompt_keys": prompt_keys, "prompt_values": prompt_values, "group_index": group_index, "prompt_length": prompt_length, "own_length": own_length, "expert_gain": expert_gain, "expert_ids": expert_ids, "expert_mix": expert_mix, "gate_weight": gate_weight, "up_weight": up_weight, "down_weight": down_weight}


epsilon = 1e-06

def rms_scale(values, gain):
    widened = values.astype(jnp.float32)
    spread = lax.optimization_barrier(jnp.mean(widened * widened, axis=-1, keepdims=True))
    return (widened * lax.rsqrt(spread + epsilon) * gain).astype(jnp.bfloat16)

def widen_rounded(values):
    return lax.optimization_barrier(values.astype(jnp.bfloat16)).astype(jnp.float32)

def attend(queries, new_keys, new_values, prompt_keys, prompt_values, group_index, prompt_length, own_length):
    layout = (REQUESTS, SB, H, HD)
    owners = jnp.arange(REQUESTS, dtype=jnp.int32) // REQ_DEV * G_DEV + group_index.reshape(-1).astype(jnp.int32)
    scale = HD ** (-0.5)
    prompt_positions = jnp.arange(PMAX, dtype=jnp.int32)
    positions = jnp.arange(SB, dtype=jnp.int32)

    def one_request(item):
        query_rows, key_rows, value_rows, owner, count = item
        group_keys = lax.dynamic_index_in_dim(prompt_keys, owner, 0, keepdims=False).reshape(PMAX, H, HD).astype(jnp.float32)
        group_values = lax.dynamic_index_in_dim(prompt_values, owner, 0, keepdims=False).reshape(PMAX, H, HD).astype(jnp.float32)
        limit = lax.dynamic_index_in_dim(prompt_length, owner, 0, keepdims=False)
        widened = query_rows.astype(jnp.float32)
        scores = jnp.einsum('ihd,jhd->hij', widened, group_keys) * scale
        scores = jnp.where(prompt_positions[None, None, :] < limit, scores, -jnp.inf)
        own_scores = jnp.einsum('ihd,jhd->hij', widened, key_rows.astype(jnp.float32)) * scale
        own_scores = jnp.where(positions[None, None, :] < count, own_scores, -jnp.inf)
        highest = jnp.maximum(lax.optimization_barrier(jnp.max(scores, axis=-1)), lax.optimization_barrier(jnp.max(own_scores, axis=-1)))
        prompt_weights = widen_rounded(jnp.exp(scores - highest[..., None]))
        own_weights = widen_rounded(jnp.exp(own_scores - highest[..., None]))
        summed = jnp.einsum('hij,jhd->ihd', prompt_weights, group_values)
        summed = summed + jnp.einsum('hij,jhd->ihd', own_weights, value_rows.astype(jnp.float32))
        totals = lax.optimization_barrier(jnp.sum(prompt_weights, axis=-1)) + lax.optimization_barrier(jnp.sum(own_weights, axis=-1))
        result = summed / jnp.transpose(totals)[..., None]
        return result.astype(jnp.bfloat16).reshape(SB, H * HD)
    items = (queries.reshape(layout), new_keys.reshape(layout), new_values.reshape(layout), owners, own_length.astype(jnp.int32))
    return lax.map(one_request, items).reshape(TOKENS, H * HD)

def experts_layer(expert_input, expert_ids, expert_mix, gate_weight, up_weight, down_weight):
    chosen = expert_ids.reshape(-1).astype(jnp.int32)
    routes = chosen.shape[0]
    owners = jnp.arange(routes, dtype=jnp.int32) // TOP
    matches = (chosen[:, None] == jnp.arange(EXPERTS, dtype=jnp.int32)[None, :]).astype(jnp.int32)
    slots = lax.optimization_barrier(jnp.sum((jnp.cumsum(matches, axis=0) - matches) * matches, axis=1)).astype(jnp.int32)
    capacity_all = N_DP * N_EXPERT * CAP
    table = jnp.full((EXPERTS, capacity_all), TOKENS, jnp.int32).at[chosen, slots].set(owners)
    shares = jnp.zeros((EXPERTS, capacity_all), jnp.float32).at[chosen, slots].set(expert_mix.reshape(-1))
    padded = jnp.concatenate([expert_input, jnp.zeros((1, D), jnp.bfloat16)], axis=0)

    def one_expert(total, expert):
        picked = table[expert]
        rows = padded[picked]
        summed = jnp.zeros((capacity_all, D), jnp.float32)
        for half in range(HSPLIT):
            shard = expert * HSPLIT + half
            gated = jnp.dot(rows, gate_weight[shard], preferred_element_type=jnp.float32)
            lifted = jnp.dot(rows, up_weight[shard], preferred_element_type=jnp.float32)
            hidden = (jax.nn.silu(gated) * lifted).astype(jnp.bfloat16)
            summed = summed + widen_rounded(jnp.dot(hidden, down_weight[shard], preferred_element_type=jnp.float32))
        total = total.at[picked].add(shares[expert][:, None] * summed, mode='drop')
        return (total, None)
    total = lax.scan(one_expert, jnp.zeros((TOKENS, D), jnp.float32), jnp.arange(EXPERTS, dtype=jnp.int32))[0]
    return total.astype(jnp.bfloat16)

def reference(residual_in, attention_gain, query_weight, key_weight, value_weight, output_weight, prompt_keys, prompt_values, group_index, prompt_length, own_length, expert_gain, expert_ids, expert_mix, gate_weight, up_weight, down_weight):
    normed = rms_scale(residual_in, attention_gain)
    queries = jnp.dot(normed, query_weight, preferred_element_type=jnp.float32).astype(jnp.bfloat16)
    new_keys = jnp.dot(normed, key_weight, preferred_element_type=jnp.float32).astype(jnp.bfloat16)
    new_values = jnp.dot(normed, value_weight, preferred_element_type=jnp.float32).astype(jnp.bfloat16)
    attended = attend(queries, new_keys, new_values, prompt_keys, prompt_values, group_index, prompt_length, own_length)
    attention_update = jnp.dot(attended, output_weight, preferred_element_type=jnp.float32).astype(jnp.bfloat16)
    expert_input = rms_scale(residual_in.astype(jnp.float32) + attention_update.astype(jnp.float32), expert_gain)
    expert_update = experts_layer(expert_input, expert_ids, expert_mix, gate_weight, up_weight, down_weight)
    return (attention_update, expert_update)
```

```python
import functools
import jax
import jax.numpy as jnp
from jax import lax
from jax.experimental import pallas as pl
from jax.experimental.pallas import tpu as pltpu
from jax.sharding import PartitionSpec as P

HD = 128
FF = 1024
TOP = 8
GSIZE = 16
SB = 32


epsilon = 1e-06


def rms_scale(values, gain):
    widened = values.astype(jnp.float32)
    spread = jnp.mean(widened * widened, axis=-1, keepdims=True)
    return (widened * lax.rsqrt(spread + epsilon) * gain).astype(jnp.bfloat16)


def expert_block(block, gate_weight, up_weight, down_weight):
    shape_kept = block.shape
    flat = block.reshape(-1, shape_kept[-1])
    gated = jnp.dot(flat, gate_weight[0], preferred_element_type=jnp.float32)
    lifted = jnp.dot(flat, up_weight[0], preferred_element_type=jnp.float32)
    hidden = (jax.nn.silu(gated) * lifted).astype(jnp.bfloat16)
    produced = jnp.dot(hidden, down_weight[0], preferred_element_type=jnp.float32).astype(
        jnp.bfloat16
    )
    return produced.reshape(shape_kept)


MESH = pl.DeviceIdType.MESH


def plane_place():
    line = lax.axis_index("dp")
    spot = lax.axis_index("expert")
    core = lax.rem(spot, 2)
    across = lax.rem(spot // 2, 2)
    upward = spot // 4
    return line, spot, core, across, upward


def greet(nz, line, spots):
    barrier = pltpu.get_barrier_semaphore()
    for other in spots:
        pl.semaphore_signal(
            barrier, inc=1, device_id={"dp": line, "expert": other}, device_id_type=MESH
        )
    if nz == 1:
        pl.semaphore_wait(barrier, len(spots))
        return
    spot = lax.axis_index("expert")

    @pl.when(line > 0)
    def _():
        pl.semaphore_signal(
            barrier, inc=1, device_id={"dp": line - 1, "expert": spot}, device_id_type=MESH
        )

    @pl.when(line < nz - 1)
    def _():
        pl.semaphore_signal(
            barrier, inc=1, device_id={"dp": line + 1, "expert": spot}, device_id_type=MESH
        )

    ends = jnp.where(line > 0, 1, 0) + jnp.where(line < nz - 1, 1, 0)
    pl.semaphore_wait(barrier, len(spots) + ends)


def gather_kernel(nz, x_ref, out_ref, local_sem, send, recv):
    line, spot, core, across, upward = plane_place()
    xn = spot + 2 - 4 * across
    yn = spot + 4 - 8 * upward
    dn = xn + yn - spot
    cn = spot + 1 - 2 * core
    zi = line if nz > 1 else 0
    rows = x_ref.shape[0]
    half = rows // 2
    whole, first, second = pl.ds(0, rows), pl.ds(0, half), pl.ds(half, half)

    def move(kind, zp, block, part, to, source=None):
        return pltpu.make_async_remote_copy(
            src_ref=out_ref.at[zp, block, part] if source is None else source,
            dst_ref=out_ref.at[zp, block, part],
            send_sem=send.at[kind, zp],
            recv_sem=recv.at[kind, zp],
            device_id={"dp": line, "expert": to},
            device_id_type=MESH,
        )

    def along(kind, zp, to, source=None):
        return pltpu.make_async_remote_copy(
            src_ref=out_ref.at[zp, spot] if source is None else source,
            dst_ref=out_ref.at[zp, spot],
            send_sem=send.at[kind, zp],
            recv_sem=recv.at[0, zp],
            device_id={"dp": to, "expert": spot},
            device_id_type=MESH,
        )

    local = pltpu.make_async_copy(x_ref, out_ref.at[zi, spot], local_sem)
    local.start()
    greet(nz, line, (xn, yn, cn))

    steps = [(0, 0)] + [(s, way) for s in range(1, nz) for way in (-1, 1)]

    def place(s, way):
        zp = zi + way * s
        valid = None if s == 0 else (zp >= 0 if way < 0 else zp <= nz - 1)
        return zp, valid

    def guarded(valid, body):
        if valid is None:
            body()
        else:
            pl.when(valid)(body)

    def begin(s, way):
        zp, valid = place(s, way)

        def body():
            source = x_ref if s == 0 else None
            if s > 0:
                along(0, zp, line).wait_recv()
            if nz > 1 and way <= 0:

                @pl.when(line < nz - 1)
                def _():
                    along(0, zp, line + 1, source).start()

            if nz > 1 and way >= 0:

                @pl.when(line > 0)
                def _():
                    along(10, zp, line - 1, source).start()

            move(1, zp, spot, whole, xn, source).start()
            move(2, zp, spot, whole, yn, source).start()
            move(5, zp, spot, whole, cn, source).start()

        guarded(valid, body)

    def middle(s, way):
        zp, valid = place(s, way)

        def body():
            move(1, zp, xn, whole, xn).wait_recv()
            move(3, zp, xn, first, yn).start()
            move(6, zp, xn, whole, cn).start()
            move(2, zp, yn, whole, yn).wait_recv()
            move(4, zp, yn, second, xn).start()
            move(7, zp, yn, whole, cn).start()

        guarded(valid, body)

    def last(s, way):
        zp, valid = place(s, way)

        def body():
            move(3, zp, dn, first, yn).wait_recv()
            move(8, zp, dn, first, cn).start()
            move(4, zp, dn, second, xn).wait_recv()
            move(9, zp, dn, second, cn).start()

        guarded(valid, body)

    for s in range(nz + 2):
        for entry in steps:
            if entry[0] == s:
                begin(*entry)
        for entry in steps:
            if entry[0] == s - 1:
                middle(*entry)
        for entry in steps:
            if entry[0] == s - 2:
                last(*entry)

    def finish(s, way):
        zp, valid = place(s, way)

        def body():
            if nz > 1 and way <= 0:

                @pl.when(line < nz - 1)
                def _():
                    along(0, zp, line + 1).wait_send()

            if nz > 1 and way >= 0:

                @pl.when(line > 0)
                def _():
                    along(10, zp, line - 1).wait_send()

            sibling = cn - spot
            for kind, block, part, to in (
                (1, spot, whole, xn),
                (2, spot, whole, yn),
                (3, xn, first, yn),
                (4, yn, second, xn),
            ):
                move(kind, zp, block, part, to).wait_send()
            for kind, block, part in (
                (5, spot, whole),
                (6, xn, whole),
                (7, yn, whole),
                (8, dn, first),
                (9, dn, second),
            ):
                move(kind, zp, block, part, cn).wait_send()
                move(kind, zp, block + sibling, part, cn).wait_recv()

        guarded(valid, body)

    for entry in steps:
        finish(*entry)
    local.wait()


def gather_rows(x, nz, number):
    rows, width = x.shape
    return pl.pallas_call(
        functools.partial(gather_kernel, nz),
        out_shape=jax.ShapeDtypeStruct((nz, 8, rows, width), x.dtype),
        in_specs=[pl.BlockSpec(memory_space=pl.ANY)],
        out_specs=pl.BlockSpec(memory_space=pl.ANY),
        scratch_shapes=[
            pltpu.SemaphoreType.DMA,
            pltpu.SemaphoreType.DMA((11, nz)),
            pltpu.SemaphoreType.DMA((10, nz)),
        ],
        compiler_params=pltpu.CompilerParams(collective_id=number, has_side_effects=True),
    )(x)


def scatter_kernel(
    nz, p_ref, out_ref, mine, sib, xa, ya, yb, xb, below, above, local, send, recv
):
    line, spot, core, across, upward = plane_place()
    xn = spot + 2 - 4 * across
    yn = spot + 4 - 8 * upward
    cn = spot + 1 - 2 * core
    zi = line if nz > 1 else 0
    rows = out_ref.shape[0]
    half = rows // 2
    first, second = pl.ds(0, half), pl.ds(half, half)
    here = 2 * upward + across
    beside = here + 1 - 2 * across
    over = here + 2 - 4 * upward
    apart = beside + over - here

    def sibling(zp, q):
        return pltpu.make_async_remote_copy(
            src_ref=p_ref.at[zp, 2 * q + 1 - core],
            dst_ref=sib.at[zp, q],
            send_sem=send.at[q, zp],
            recv_sem=recv.at[q, zp],
            device_id={"dp": line, "expert": cn},
            device_id_type=MESH,
        )

    def own(zp, q):
        return pltpu.make_async_copy(
            p_ref.at[zp, 2 * q + core], mine.at[zp, q], local.at[q, zp]
        )

    def plane(kind, zp, source, target, to):
        return pltpu.make_async_remote_copy(
            src_ref=source,
            dst_ref=target,
            send_sem=send.at[kind, zp],
            recv_sem=recv.at[kind, zp],
            device_id={"dp": line, "expert": to},
            device_id_type=MESH,
        )

    def early(zp):
        return (
            plane(4, zp, mine.at[zp, apart, first], xa.at[zp, 1], xn),
            plane(5, zp, mine.at[zp, apart, second], ya.at[zp, 1], yn),
            plane(6, zp, mine.at[zp, beside, first], xa.at[zp, 0], xn),
            plane(7, zp, mine.at[zp, over, second], ya.at[zp, 0], yn),
        )

    def late(zp):
        return (
            plane(8, zp, mine.at[zp, over, first], yb.at[zp], yn),
            plane(9, zp, mine.at[zp, beside, second], xb.at[zp], xn),
        )

    def upwards(zp, to):
        return pltpu.make_async_remote_copy(
            src_ref=mine.at[zp, here],
            dst_ref=below.at[zp],
            send_sem=send.at[10, zp],
            recv_sem=recv.at[10, zp],
            device_id={"dp": to, "expert": spot},
            device_id_type=MESH,
        )

    def downwards(zp, to):
        return pltpu.make_async_remote_copy(
            src_ref=mine.at[zp, here],
            dst_ref=above.at[zp],
            send_sem=send.at[11, zp],
            recv_sem=recv.at[11, zp],
            device_id={"dp": to, "expert": spot},
            device_id_type=MESH,
        )

    def add(zp, q, start, count, other):
        step = 16

        def body(i, carry):
            r = pl.multiple_of(i * step, step)
            target = mine.at[zp, q, pl.ds(start + r, step)]
            total = target[...].astype(jnp.float32) + other[pl.ds(r, step)].astype(jnp.float32)
            target[...] = total.astype(jnp.bfloat16)
            return carry

        lax.fori_loop(0, count // step, body, 0)

    if nz > 1:
        low = line < nz // 2
        order = [jnp.where(low, nz - 1 - k, k) for k in range(nz)]
    else:
        order = [0]
    sequence = (apart, beside, over, here)
    for zp in order:
        for q in sequence:
            own(zp, q).start()
    greet(nz, line, (xn, yn, cn))
    for zp in order:
        for q in sequence:
            sibling(zp, q).start()

    def stage_one(zp):
        for q in sequence:
            own(zp, q).wait()
            sibling(zp, q).wait_recv()
            add(zp, q, 0, rows, sib.at[zp, q])
            if q is apart:
                early(zp)[0].start()
                early(zp)[1].start()
            elif q is beside:
                early(zp)[2].start()
            elif q is over:
                early(zp)[3].start()

    def stage_two(zp):
        copies = early(zp)
        copies[0].wait_recv()
        add(zp, over, 0, half, xa.at[zp, 1])
        late(zp)[0].start()
        copies[1].wait_recv()
        copies[2].wait_recv()
        add(zp, here, 0, half, xa.at[zp, 0])
        copies[3].wait_recv()
        add(zp, here, half, half, ya.at[zp, 0])
        add(zp, beside, half, half, ya.at[zp, 1])
        late(zp)[1].start()

    def stage_three(zp):
        copies = late(zp)
        copies[0].wait_recv()
        add(zp, here, 0, half, yb.at[zp])
        copies[1].wait_recv()
        add(zp, here, half, half, xb.at[zp])
        if nz > 1:

            @pl.when((zp >= line) & (line > 0))
            def _():
                upwards(zp, line).wait_recv()
                add(zp, here, 0, rows, below.at[zp])

            @pl.when((zp <= line) & (line < nz - 1))
            def _():
                downwards(zp, line).wait_recv()
                add(zp, here, 0, rows, above.at[zp])

            @pl.when(zp > line)
            def _():
                upwards(zp, line + 1).start()

            @pl.when(zp < line)
            def _():
                downwards(zp, line - 1).start()

    for k in range(nz + 2):
        if k < nz:
            stage_one(order[k])
        if 0 <= k - 1 < nz:
            stage_two(order[k - 1])
        if 0 <= k - 2 < nz:
            stage_three(order[k - 2])
    out_ref[...] = mine[zi, here]
    for zp in order:
        for q in sequence:
            sibling(zp, q).wait_send()
        for copy in early(zp) + late(zp):
            copy.wait_send()
        if nz > 1:

            @pl.when(zp > line)
            def _():
                upwards(zp, line + 1).wait_send()

            @pl.when(zp < line)
            def _():
                downwards(zp, line - 1).wait_send()


def scatter_sum(p, number):
    nz, _, rows, width = p.shape
    half = rows // 2
    kind = p.dtype
    return pl.pallas_call(
        functools.partial(scatter_kernel, nz),
        out_shape=jax.ShapeDtypeStruct((rows, width), kind),
        in_specs=[pl.BlockSpec(memory_space=pl.ANY)],
        out_specs=pl.BlockSpec(memory_space=pltpu.VMEM),
        scratch_shapes=[
            pltpu.VMEM((nz, 4, rows, width), kind),
            pltpu.VMEM((nz, 4, rows, width), kind),
            pltpu.VMEM((nz, 2, half, width), kind),
            pltpu.VMEM((nz, 2, half, width), kind),
            pltpu.VMEM((nz, half, width), kind),
            pltpu.VMEM((nz, half, width), kind),
            pltpu.VMEM((nz, rows, width), kind),
            pltpu.VMEM((nz, rows, width), kind),
            pltpu.SemaphoreType.DMA((4, nz)),
            pltpu.SemaphoreType.DMA((12, nz)),
            pltpu.SemaphoreType.DMA((12, nz)),
        ],
        compiler_params=pltpu.CompilerParams(
            collective_id=number, has_side_effects=True, vmem_limit_bytes=48 * 2**20
        ),
    )(p)


def expert_kernel(capacity, x_ref, slot_ref, share_ref, gate_ref, up_ref, down_ref, out_ref, rows):
    blocks, tokens, width = x_ref.shape[1:]
    spots = lax.broadcasted_iota(jnp.int32, (capacity, tokens), 0)

    def select(b):
        return jnp.where(spots == slot_ref[0, b : b + 1, :], 1.0, 0.0).astype(jnp.bfloat16)

    for b in range(blocks):
        rows[b * capacity : (b + 1) * capacity, :] = jnp.dot(
            select(b), x_ref[0, b], preferred_element_type=jnp.float32
        ).astype(jnp.bfloat16)
    flat = rows[...]
    gated = jnp.dot(flat, gate_ref[0], preferred_element_type=jnp.float32)
    lifted = jnp.dot(flat, up_ref[0], preferred_element_type=jnp.float32)
    hidden = (gated / (1.0 + jnp.exp(-gated)) * lifted).astype(jnp.bfloat16)
    rows[...] = jnp.dot(hidden, down_ref[0], preferred_element_type=jnp.float32).astype(
        jnp.bfloat16
    )
    for b in range(blocks):
        spread = lax.dot_general(
            select(b),
            rows[b * capacity : (b + 1) * capacity, :],
            (((0,), (0,)), ((), ())),
            preferred_element_type=jnp.float32,
        )
        out_ref[0, b] = (spread * share_ref[0, b]).astype(jnp.bfloat16)


def expert_partials(x, slots, shares, gate_weight, up_weight, down_weight, capacity):
    nz, blocks, tokens, width = x.shape
    hidden_units = gate_weight.shape[2]
    once = pl.Buffered(1)
    return pl.pallas_call(
        functools.partial(expert_kernel, capacity),
        grid=(nz,),
        out_shape=jax.ShapeDtypeStruct(x.shape, jnp.bfloat16),
        in_specs=[
            pl.BlockSpec((1, blocks, tokens, width), lambda i: (i, 0, 0, 0)),
            pl.BlockSpec((1, blocks, tokens), lambda i: (i, 0, 0)),
            pl.BlockSpec((1, blocks, tokens, 1), lambda i: (i, 0, 0, 0)),
            pl.BlockSpec((1, width, hidden_units), lambda i: (0, 0, 0), pipeline_mode=once),
            pl.BlockSpec((1, width, hidden_units), lambda i: (0, 0, 0), pipeline_mode=once),
            pl.BlockSpec((1, hidden_units, width), lambda i: (0, 0, 0), pipeline_mode=once),
        ],
        out_specs=pl.BlockSpec((1, blocks, tokens, width), lambda i: (i, 0, 0, 0)),
        scratch_shapes=[pltpu.VMEM((blocks * capacity, width), jnp.bfloat16)],
        compiler_params=pltpu.CompilerParams(vmem_limit_bytes=52 * 2**20),
        cost_estimate=pl.CostEstimate(
            flops=6 * nz * blocks * capacity * width * hidden_units,
            bytes_accessed=4 * nz * blocks * tokens * width,
            transcendentals=0,
        ),
    )(x, slots, shares, gate_weight, up_weight, down_weight)


def experts_by_plane(expert_input, expert_ids, expert_mix, gate_weight, up_weight, down_weight):
    tok_rows = expert_input.shape[0]
    nz, spots = lax.axis_size("dp"), lax.axis_size("expert")
    devices = nz * spots
    capacity = max(2, tok_rows * TOP * 3 // (2 * devices))
    ids = lax.all_gather(expert_ids, ("dp", "expert"), axis=0, tiled=True)
    mix = lax.all_gather(expert_mix, ("dp", "expert"), axis=0, tiled=True)
    me = lax.axis_index("dp") * spots + lax.axis_index("expert")
    named = ids == me
    hit = jnp.any(named, axis=1).reshape(devices, tok_rows)
    shares = jnp.sum(jnp.where(named, mix, 0.0), axis=1).reshape(nz, spots, tok_rows, 1)
    before = jnp.triu(jnp.ones((tok_rows, tok_rows), jnp.bfloat16), 1)
    slots = jnp.dot(hit.astype(jnp.bfloat16), before, preferred_element_type=jnp.float32)
    slots = jnp.where(hit, slots.astype(jnp.int32), -1).reshape(nz, spots, tok_rows)
    gathered = gather_rows(expert_input, nz, 2)
    partials = expert_partials(
        gathered, slots, shares, gate_weight, up_weight, down_weight, capacity
    )
    return scatter_sum(partials, 3)


def per_device(
    residual_in,
    attention_gain,
    query_weight,
    key_weight,
    value_weight,
    output_weight,
    prompt_keys,
    prompt_values,
    group_index,
    prompt_length,
    own_length,
    expert_gain,
    expert_ids,
    expert_mix,
    gate_weight,
    up_weight,
    down_weight,
):
    tok_rows, width = residual_in.shape
    local_width = query_weight.shape[1]
    heads_here = local_width // HD
    requests = group_index.shape[1]
    longest = prompt_keys.shape[1]
    groups_here = prompt_keys.shape[0]
    normed = rms_scale(residual_in, attention_gain)
    planar = lax.axis_size("expert") == 8 and gate_weight.shape[2] == FF
    if planar:
        piece = gather_rows(normed, 1, 0).reshape(-1, width)
    else:
        piece = lax.all_gather(normed, "expert", axis=0, tiled=True)
    query_part = jnp.dot(piece, query_weight, preferred_element_type=jnp.float32).astype(
        jnp.bfloat16
    )
    key_part = jnp.dot(piece, key_weight, preferred_element_type=jnp.float32).astype(jnp.bfloat16)
    value_part = jnp.dot(piece, value_weight, preferred_element_type=jnp.float32).astype(
        jnp.bfloat16
    )
    projected = jnp.concatenate([query_part, key_part, value_part], axis=1)
    layout = (requests, SB, heads_here, HD)
    queries = projected[:, :local_width].reshape(layout)
    new_keys = projected[:, local_width : 2 * local_width].reshape(layout)
    new_values = projected[:, 2 * local_width :].reshape(layout)
    scale = HD ** (-0.5)
    positions = jnp.arange(SB, dtype=jnp.int32)
    own_scores = (
        jnp.einsum("rihd,rjhd->rhij", queries, new_keys, preferred_element_type=jnp.float32) * scale
    )
    own_scores = jnp.where(
        positions[None, None, None, :] < own_length[:, None, None, None], own_scores, -jnp.inf
    )
    member = group_index[0]
    prompt_positions = jnp.arange(longest, dtype=jnp.int32)

    def group_step(group, attended):
        first = jnp.sum((member < group).astype(jnp.int32))
        start = jnp.minimum(first, requests - GSIZE)
        window_queries = lax.dynamic_slice_in_dim(queries, start, GSIZE, 0)
        group_keys = lax.dynamic_index_in_dim(prompt_keys, group, 0, keepdims=False).reshape(
            longest, heads_here, HD
        )
        group_values = lax.dynamic_index_in_dim(prompt_values, group, 0, keepdims=False).reshape(
            longest, heads_here, HD
        )
        scores = (
            jnp.einsum(
                "rihd,jhd->rhij", window_queries, group_keys, preferred_element_type=jnp.float32
            )
            * scale
        )
        limit = lax.dynamic_index_in_dim(prompt_length, group, 0, keepdims=False)
        scores = jnp.where(prompt_positions < limit, scores, -jnp.inf)
        window_own = lax.dynamic_slice_in_dim(own_scores, start, GSIZE, 0)
        highest = jnp.maximum(jnp.max(scores, axis=-1), jnp.max(window_own, axis=-1))
        prompt_weights = jnp.exp(scores - highest[..., None]).astype(jnp.bfloat16)
        own_weights = jnp.exp(window_own - highest[..., None]).astype(jnp.bfloat16)
        window_values = lax.dynamic_slice_in_dim(new_values, start, GSIZE, 0)
        summed = jnp.einsum(
            "rhij,jhd->rihd", prompt_weights, group_values, preferred_element_type=jnp.float32
        )
        summed = summed + jnp.einsum(
            "rhij,rjhd->rihd", own_weights, window_values, preferred_element_type=jnp.float32
        )
        totals = jnp.sum(prompt_weights, axis=-1, dtype=jnp.float32) + jnp.sum(
            own_weights, axis=-1, dtype=jnp.float32
        )
        result = (summed / jnp.transpose(totals, (0, 2, 1))[..., None]).astype(jnp.bfloat16)
        inside = lax.dynamic_slice_in_dim(member, start, GSIZE, 0) == group
        current = lax.dynamic_slice_in_dim(attended, start, GSIZE, 0)
        merged = jnp.where(inside[:, None, None, None], result, current)
        return lax.dynamic_update_slice_in_dim(attended, merged, start, 0)

    attended = lax.fori_loop(0, groups_here, group_step, jnp.zeros(layout, jnp.bfloat16))
    flat_attended = attended.reshape(requests * SB, local_width)
    piece = flat_attended
    update_part = jnp.dot(piece, output_weight, preferred_element_type=jnp.float32).astype(
        jnp.bfloat16
    )
    if planar:
        attention_update = scatter_sum(update_part.reshape(1, 8, tok_rows, width), 1)
    else:
        attention_update = lax.psum_scatter(
            update_part, "expert", scatter_dimension=0, tiled=True
        )
    expert_input = rms_scale(
        residual_in.astype(jnp.float32) + attention_update.astype(jnp.float32), expert_gain
    )
    if planar:
        expert_update = experts_by_plane(
            expert_input, expert_ids, expert_mix, gate_weight, up_weight, down_weight
        )
        return (attention_update, expert_update)
    data_groups = lax.axis_size("dp")
    expert_groups = lax.axis_size("expert")
    devices = data_groups * expert_groups
    hidden_split = FF // gate_weight.shape[2]
    experts = devices // hidden_split
    capacity = max(2, tok_rows * TOP * 3 // (2 * experts))
    chosen = expert_ids.reshape(-1)
    routes_here = chosen.shape[0]
    owners = jnp.arange(routes_here, dtype=jnp.int32) // TOP
    matches = (chosen[:, None] == jnp.arange(experts, dtype=jnp.int32)[None, :]).astype(jnp.int32)
    slots = jnp.sum((jnp.cumsum(matches, axis=0) - matches) * matches, axis=1)
    table = (
        jnp.full((experts * capacity,), tok_rows, jnp.int32)
        .at[chosen * capacity + slots]
        .set(owners)
    )
    padded = jnp.concatenate([expert_input, jnp.zeros((1, width), jnp.bfloat16)], axis=0)
    outgoing = jnp.broadcast_to(
        padded[table].reshape(experts, 1, capacity, width), (experts, hidden_split, capacity, width)
    )
    outgoing = outgoing.reshape(devices, capacity, width)
    returned = lax.all_to_all(
        expert_block(
            lax.all_to_all(outgoing, ("dp", "expert"), split_axis=0, concat_axis=0, tiled=True),
            gate_weight,
            up_weight,
            down_weight,
        ),
        ("dp", "expert"),
        split_axis=0,
        concat_axis=0,
        tiled=True,
    )
    pieces = returned.reshape(experts, hidden_split, capacity, width)[chosen, :, slots]
    blended = jnp.sum(pieces.astype(jnp.float32), axis=1) * expert_mix.reshape(-1)[:, None]
    expert_update = jnp.sum(blended.reshape(tok_rows, TOP, width), axis=1).astype(jnp.bfloat16)
    return (attention_update, expert_update)


def solution(mesh):
    in_specs = (
        P(("dp", "expert"), None),
        P(),
        P(None, "expert"),
        P(None, "expert"),
        P(None, "expert"),
        P("expert", None),
        P("dp", None, "expert"),
        P("dp", None, "expert"),
        P("dp", None),
        P("dp"),
        P("dp"),
        P(),
        P(("dp", "expert"), None),
        P(("dp", "expert"), None),
        P(("dp", "expert"), None, None),
        P(("dp", "expert"), None, None),
        P(("dp", "expert"), None, None),
    )
    out_specs = (P(("dp", "expert"), None), P(("dp", "expert"), None))
    return jax.shard_map(
        per_device, mesh=mesh, in_specs=in_specs, out_specs=out_specs, check_vma=False
    )
```

```python
import functools
import jax
import jax.numpy as jnp
from jax import lax
from jax.experimental import pallas as pl
from jax.experimental.pallas import tpu as pltpu
from jax.sharding import PartitionSpec as P

HD = 128
FF = 1024
TOP = 8
GSIZE = 16
SB = 32


epsilon = 1e-06


def rms_scale(values, gain):
    widened = values.astype(jnp.float32)
    spread = jnp.mean(widened * widened, axis=-1, keepdims=True)
    return (widened * lax.rsqrt(spread + epsilon) * gain).astype(jnp.bfloat16)


def expert_block(block, gate_weight, up_weight, down_weight):
    shape_kept = block.shape
    flat = block.reshape(-1, shape_kept[-1])
    gated = jnp.dot(flat, gate_weight[0], preferred_element_type=jnp.float32)
    lifted = jnp.dot(flat, up_weight[0], preferred_element_type=jnp.float32)
    hidden = (jax.nn.silu(gated) * lifted).astype(jnp.bfloat16)
    produced = jnp.dot(hidden, down_weight[0], preferred_element_type=jnp.float32).astype(
        jnp.bfloat16
    )
    return produced.reshape(shape_kept)


MESH = pl.DeviceIdType.MESH


def plane_place():
    line = lax.axis_index("dp")
    spot = lax.axis_index("expert")
    core = lax.rem(spot, 2)
    across = lax.rem(spot // 2, 2)
    upward = spot // 4
    return line, spot, core, across, upward


def greet(nz, line, spots):
    barrier = pltpu.get_barrier_semaphore()
    for other in spots:
        pl.semaphore_signal(
            barrier, inc=1, device_id={"dp": line, "expert": other}, device_id_type=MESH
        )
    if nz == 1:
        pl.semaphore_wait(barrier, len(spots))
        return
    spot = lax.axis_index("expert")

    @pl.when(line > 0)
    def _():
        pl.semaphore_signal(
            barrier, inc=1, device_id={"dp": line - 1, "expert": spot}, device_id_type=MESH
        )

    @pl.when(line < nz - 1)
    def _():
        pl.semaphore_signal(
            barrier, inc=1, device_id={"dp": line + 1, "expert": spot}, device_id_type=MESH
        )

    ends = jnp.where(line > 0, 1, 0) + jnp.where(line < nz - 1, 1, 0)
    pl.semaphore_wait(barrier, len(spots) + ends)


def gather_kernel(nz, x_ref, out_ref, local_sem, send, recv):
    line, spot, core, across, upward = plane_place()
    xn = spot + 2 - 4 * across
    yn = spot + 4 - 8 * upward
    dn = xn + yn - spot
    cn = spot + 1 - 2 * core
    zi = line if nz > 1 else 0
    rows = x_ref.shape[0]
    half = rows // 2
    whole, first, second = pl.ds(0, rows), pl.ds(0, half), pl.ds(half, half)

    def move(kind, zp, block, part, to, source=None):
        return pltpu.make_async_remote_copy(
            src_ref=out_ref.at[zp, block, part] if source is None else source,
            dst_ref=out_ref.at[zp, block, part],
            send_sem=send.at[kind, zp],
            recv_sem=recv.at[kind, zp],
            device_id={"dp": line, "expert": to},
            device_id_type=MESH,
        )

    def along(kind, zp, to, source=None):
        return pltpu.make_async_remote_copy(
            src_ref=out_ref.at[zp, spot] if source is None else source,
            dst_ref=out_ref.at[zp, spot],
            send_sem=send.at[kind, zp],
            recv_sem=recv.at[0, zp],
            device_id={"dp": to, "expert": spot},
            device_id_type=MESH,
        )

    local = pltpu.make_async_copy(x_ref, out_ref.at[zi, spot], local_sem)
    local.start()
    greet(nz, line, (xn, yn, cn))

    steps = [(0, 0)] + [(s, way) for s in range(1, nz) for way in (-1, 1)]

    def place(s, way):
        zp = zi + way * s
        valid = None if s == 0 else (zp >= 0 if way < 0 else zp <= nz - 1)
        return zp, valid

    def guarded(valid, body):
        if valid is None:
            body()
        else:
            pl.when(valid)(body)

    def begin(s, way):
        zp, valid = place(s, way)

        def body():
            source = x_ref if s == 0 else None
            if s > 0:
                along(0, zp, line).wait_recv()
            if nz > 1 and way <= 0:

                @pl.when(line < nz - 1)
                def _():
                    along(0, zp, line + 1, source).start()

            if nz > 1 and way >= 0:

                @pl.when(line > 0)
                def _():
                    along(10, zp, line - 1, source).start()

            move(1, zp, spot, whole, xn, source).start()
            move(2, zp, spot, whole, yn, source).start()
            move(5, zp, spot, whole, cn, source).start()

        guarded(valid, body)

    def middle(s, way):
        zp, valid = place(s, way)

        def body():
            move(1, zp, xn, whole, xn).wait_recv()
            move(3, zp, xn, first, yn).start()
            move(6, zp, xn, whole, cn).start()
            move(2, zp, yn, whole, yn).wait_recv()
            move(4, zp, yn, second, xn).start()
            move(7, zp, yn, whole, cn).start()

        guarded(valid, body)

    def last(s, way):
        zp, valid = place(s, way)

        def body():
            move(3, zp, dn, first, yn).wait_recv()
            move(8, zp, dn, first, cn).start()
            move(4, zp, dn, second, xn).wait_recv()
            move(9, zp, dn, second, cn).start()

        guarded(valid, body)

    for s in range(nz + 2):
        for entry in steps:
            if entry[0] == s:
                begin(*entry)
        for entry in steps:
            if entry[0] == s - 1:
                middle(*entry)
        for entry in steps:
            if entry[0] == s - 2:
                last(*entry)

    def finish(s, way):
        zp, valid = place(s, way)

        def body():
            if nz > 1 and way <= 0:

                @pl.when(line < nz - 1)
                def _():
                    along(0, zp, line + 1).wait_send()

            if nz > 1 and way >= 0:

                @pl.when(line > 0)
                def _():
                    along(10, zp, line - 1).wait_send()

            sibling = cn - spot
            for kind, block, part, to in (
                (1, spot, whole, xn),
                (2, spot, whole, yn),
                (3, xn, first, yn),
                (4, yn, second, xn),
            ):
                move(kind, zp, block, part, to).wait_send()
            for kind, block, part in (
                (5, spot, whole),
                (6, xn, whole),
                (7, yn, whole),
                (8, dn, first),
                (9, dn, second),
            ):
                move(kind, zp, block, part, cn).wait_send()
                move(kind, zp, block + sibling, part, cn).wait_recv()

        guarded(valid, body)

    for entry in steps:
        finish(*entry)
    local.wait()


def gather_rows(x, nz, number):
    rows, width = x.shape
    return pl.pallas_call(
        functools.partial(gather_kernel, nz),
        out_shape=jax.ShapeDtypeStruct((nz, 8, rows, width), x.dtype),
        in_specs=[pl.BlockSpec(memory_space=pl.ANY)],
        out_specs=pl.BlockSpec(memory_space=pl.ANY),
        scratch_shapes=[
            pltpu.SemaphoreType.DMA,
            pltpu.SemaphoreType.DMA((11, nz)),
            pltpu.SemaphoreType.DMA((10, nz)),
        ],
        compiler_params=pltpu.CompilerParams(collective_id=number, has_side_effects=True),
    )(x)


def scatter_kernel(
    nz, p_ref, out_ref, mine, sib, xa, ya, yb, xb, below, above, local, send, recv
):
    line, spot, core, across, upward = plane_place()
    xn = spot + 2 - 4 * across
    yn = spot + 4 - 8 * upward
    cn = spot + 1 - 2 * core
    zi = line if nz > 1 else 0
    rows = out_ref.shape[0]
    half = rows // 2
    first, second = pl.ds(0, half), pl.ds(half, half)
    here = 2 * upward + across
    beside = here + 1 - 2 * across
    over = here + 2 - 4 * upward
    apart = beside + over - here

    def sibling(zp, q):
        return pltpu.make_async_remote_copy(
            src_ref=p_ref.at[zp, 2 * q + 1 - core],
            dst_ref=sib.at[zp, q],
            send_sem=send.at[q, zp],
            recv_sem=recv.at[q, zp],
            device_id={"dp": line, "expert": cn},
            device_id_type=MESH,
        )

    def own(zp, q):
        return pltpu.make_async_copy(
            p_ref.at[zp, 2 * q + core], mine.at[zp, q], local.at[q, zp]
        )

    def plane(kind, zp, source, target, to):
        return pltpu.make_async_remote_copy(
            src_ref=source,
            dst_ref=target,
            send_sem=send.at[kind, zp],
            recv_sem=recv.at[kind, zp],
            device_id={"dp": line, "expert": to},
            device_id_type=MESH,
        )

    def early(zp):
        return (
            plane(4, zp, mine.at[zp, apart, first], xa.at[zp, 1], xn),
            plane(5, zp, mine.at[zp, apart, second], ya.at[zp, 1], yn),
            plane(6, zp, mine.at[zp, beside, first], xa.at[zp, 0], xn),
            plane(7, zp, mine.at[zp, over, second], ya.at[zp, 0], yn),
        )

    def late(zp):
        return (
            plane(8, zp, mine.at[zp, over, first], yb.at[zp], yn),
            plane(9, zp, mine.at[zp, beside, second], xb.at[zp], xn),
        )

    def upwards(zp, to):
        return pltpu.make_async_remote_copy(
            src_ref=mine.at[zp, here],
            dst_ref=below.at[zp],
            send_sem=send.at[10, zp],
            recv_sem=recv.at[10, zp],
            device_id={"dp": to, "expert": spot},
            device_id_type=MESH,
        )

    def downwards(zp, to):
        return pltpu.make_async_remote_copy(
            src_ref=mine.at[zp, here],
            dst_ref=above.at[zp],
            send_sem=send.at[11, zp],
            recv_sem=recv.at[11, zp],
            device_id={"dp": to, "expert": spot},
            device_id_type=MESH,
        )

    def add(zp, q, start, count, other):
        step = 16

        def body(i, carry):
            r = pl.multiple_of(i * step, step)
            target = mine.at[zp, q, pl.ds(start + r, step)]
            total = target[...].astype(jnp.float32) + other[pl.ds(r, step)].astype(jnp.float32)
            target[...] = total.astype(jnp.bfloat16)
            return carry

        lax.fori_loop(0, count // step, body, 0)

    if nz > 1:
        low = line < nz // 2
        order = [jnp.where(low, nz - 1 - k, k) for k in range(nz)]
    else:
        order = [0]
    sequence = (apart, beside, over, here)
    for zp in order:
        for q in sequence:
            own(zp, q).start()
    greet(nz, line, (xn, yn, cn))
    for zp in order:
        for q in sequence:
            sibling(zp, q).start()

    def stage_one(zp):
        for q in sequence:
            own(zp, q).wait()
            sibling(zp, q).wait_recv()
            add(zp, q, 0, rows, sib.at[zp, q])
            if q is apart:
                early(zp)[0].start()
                early(zp)[1].start()
            elif q is beside:
                early(zp)[2].start()
            elif q is over:
                early(zp)[3].start()

    def stage_two(zp):
        copies = early(zp)
        copies[0].wait_recv()
        add(zp, over, 0, half, xa.at[zp, 1])
        late(zp)[0].start()
        copies[1].wait_recv()
        copies[2].wait_recv()
        add(zp, here, 0, half, xa.at[zp, 0])
        copies[3].wait_recv()
        add(zp, here, half, half, ya.at[zp, 0])
        add(zp, beside, half, half, ya.at[zp, 1])
        late(zp)[1].start()

    def stage_three(zp):
        copies = late(zp)
        copies[0].wait_recv()
        add(zp, here, 0, half, yb.at[zp])
        copies[1].wait_recv()
        add(zp, here, half, half, xb.at[zp])
        if nz > 1:

            @pl.when((zp >= line) & (line > 0))
            def _():
                upwards(zp, line).wait_recv()
                add(zp, here, 0, rows, below.at[zp])

            @pl.when((zp <= line) & (line < nz - 1))
            def _():
                downwards(zp, line).wait_recv()
                add(zp, here, 0, rows, above.at[zp])

            @pl.when(zp > line)
            def _():
                upwards(zp, line + 1).start()

            @pl.when(zp < line)
            def _():
                downwards(zp, line - 1).start()

    for k in range(nz + 2):
        if k < nz:
            stage_one(order[k])
        if 0 <= k - 1 < nz:
            stage_two(order[k - 1])
        if 0 <= k - 2 < nz:
            stage_three(order[k - 2])
    out_ref[...] = mine[zi, here]
    for zp in order:
        for q in sequence:
            sibling(zp, q).wait_send()
        for copy in early(zp) + late(zp):
            copy.wait_send()
        if nz > 1:

            @pl.when(zp > line)
            def _():
                upwards(zp, line + 1).wait_send()

            @pl.when(zp < line)
            def _():
                downwards(zp, line - 1).wait_send()


def scatter_sum(p, number):
    nz, _, rows, width = p.shape
    half = rows // 2
    kind = p.dtype
    return pl.pallas_call(
        functools.partial(scatter_kernel, nz),
        out_shape=jax.ShapeDtypeStruct((rows, width), kind),
        in_specs=[pl.BlockSpec(memory_space=pl.ANY)],
        out_specs=pl.BlockSpec(memory_space=pltpu.VMEM),
        scratch_shapes=[
            pltpu.VMEM((nz, 4, rows, width), kind),
            pltpu.VMEM((nz, 4, rows, width), kind),
            pltpu.VMEM((nz, 2, half, width), kind),
            pltpu.VMEM((nz, 2, half, width), kind),
            pltpu.VMEM((nz, half, width), kind),
            pltpu.VMEM((nz, half, width), kind),
            pltpu.VMEM((nz, rows, width), kind),
            pltpu.VMEM((nz, rows, width), kind),
            pltpu.SemaphoreType.DMA((4, nz)),
            pltpu.SemaphoreType.DMA((12, nz)),
            pltpu.SemaphoreType.DMA((12, nz)),
        ],
        compiler_params=pltpu.CompilerParams(
            collective_id=number, has_side_effects=True, vmem_limit_bytes=48 * 2**20
        ),
    )(p)


def expert_kernel(capacity, x_ref, gate_ref, up_ref, down_ref, out_ref, rows):
    blocks, tokens = x_ref.shape[1:3]
    width = out_ref.shape[3]
    me = lax.axis_index("dp") * blocks + lax.axis_index("expert")
    spots = lax.broadcasted_iota(jnp.int32, (tokens, capacity), 1).astype(jnp.float32)
    earlier = lax.broadcasted_iota(jnp.int32, (tokens, tokens), 1)
    earlier = earlier < lax.broadcasted_iota(jnp.int32, (tokens, tokens), 0)
    earlier = jnp.where(earlier, 1.0, 0.0).astype(jnp.bfloat16)
    mine = me.astype(jnp.float32)
    places, shares = [], []
    for b in range(blocks):
        extra = x_ref[0, b, :, width:].astype(jnp.float32)
        named = extra[:, :TOP] == mine
        mix = extra[:, TOP : 2 * TOP] + extra[:, 2 * TOP : 3 * TOP]
        mix = mix + extra[:, 3 * TOP : 4 * TOP]
        shares.append(jnp.sum(jnp.where(named, mix, 0.0), axis=1, keepdims=True))
        hit = jnp.sum(jnp.where(named, 1.0, 0.0), axis=1, keepdims=True)
        hit = jnp.broadcast_to(hit, (tokens, capacity))
        slots = jnp.dot(earlier, hit.astype(jnp.bfloat16), preferred_element_type=jnp.float32)
        place = jnp.where((hit > 0.5) & (slots == spots), 1.0, 0.0).astype(jnp.bfloat16)
        places.append(place)
        rows[b * capacity : (b + 1) * capacity, :] = lax.dot_general(
            place,
            x_ref[0, b, :, :width],
            (((0,), (0,)), ((), ())),
            preferred_element_type=jnp.float32,
        ).astype(jnp.bfloat16)
    flat = rows[...]
    gated = jnp.dot(flat, gate_ref[0], preferred_element_type=jnp.float32)
    lifted = jnp.dot(flat, up_ref[0], preferred_element_type=jnp.float32)
    hidden = (gated / (1.0 + jnp.exp(-gated)) * lifted).astype(jnp.bfloat16)
    rows[...] = jnp.dot(hidden, down_ref[0], preferred_element_type=jnp.float32).astype(
        jnp.bfloat16
    )
    for b in range(blocks):
        spread = jnp.dot(
            places[b],
            rows[b * capacity : (b + 1) * capacity, :],
            preferred_element_type=jnp.float32,
        )
        out_ref[0, b] = (spread * shares[b]).astype(jnp.bfloat16)


def expert_partials(x, gate_weight, up_weight, down_weight, capacity):
    nz, blocks, tokens, wide = x.shape
    width = gate_weight.shape[1]
    hidden_units = gate_weight.shape[2]
    once = pl.Buffered(1)
    return pl.pallas_call(
        functools.partial(expert_kernel, capacity),
        grid=(nz,),
        out_shape=jax.ShapeDtypeStruct((nz, blocks, tokens, width), jnp.bfloat16),
        in_specs=[
            pl.BlockSpec((1, blocks, tokens, wide), lambda i: (i, 0, 0, 0)),
            pl.BlockSpec((1, width, hidden_units), lambda i: (0, 0, 0), pipeline_mode=once),
            pl.BlockSpec((1, width, hidden_units), lambda i: (0, 0, 0), pipeline_mode=once),
            pl.BlockSpec((1, hidden_units, width), lambda i: (0, 0, 0), pipeline_mode=once),
        ],
        out_specs=pl.BlockSpec((1, blocks, tokens, width), lambda i: (i, 0, 0, 0)),
        scratch_shapes=[pltpu.VMEM((blocks * capacity, width), jnp.bfloat16)],
        compiler_params=pltpu.CompilerParams(vmem_limit_bytes=52 * 2**20),
        cost_estimate=pl.CostEstimate(
            flops=6 * nz * blocks * capacity * width * hidden_units,
            bytes_accessed=4 * nz * blocks * tokens * width,
            transcendentals=0,
        ),
    )(x, gate_weight, up_weight, down_weight)


def experts_by_plane(expert_input, expert_ids, expert_mix, gate_weight, up_weight, down_weight):
    tok_rows = expert_input.shape[0]
    nz, spots = lax.axis_size("dp"), lax.axis_size("expert")
    devices = nz * spots
    capacity = max(2, tok_rows * TOP * 3 // (2 * devices))
    high = lax.reduce_precision(expert_mix, 8, 7)
    middle = lax.reduce_precision(expert_mix - high, 8, 7)
    low = expert_mix - high - middle
    routes = jnp.concatenate(
        [part.astype(jnp.bfloat16) for part in (expert_ids, high, middle, low)], axis=1
    )
    routes = jnp.pad(routes, ((0, 0), (0, 128 - routes.shape[1])))
    gathered = gather_rows(jnp.concatenate([expert_input, routes], axis=1), nz, 2)
    partials = expert_partials(gathered, gate_weight, up_weight, down_weight, capacity)
    return scatter_sum(partials, 3)


def per_device(
    residual_in,
    attention_gain,
    query_weight,
    key_weight,
    value_weight,
    output_weight,
    prompt_keys,
    prompt_values,
    group_index,
    prompt_length,
    own_length,
    expert_gain,
    expert_ids,
    expert_mix,
    gate_weight,
    up_weight,
    down_weight,
):
    tok_rows, width = residual_in.shape
    local_width = query_weight.shape[1]
    heads_here = local_width // HD
    requests = group_index.shape[1]
    longest = prompt_keys.shape[1]
    groups_here = prompt_keys.shape[0]
    normed = rms_scale(residual_in, attention_gain)
    planar = lax.axis_size("expert") == 8 and gate_weight.shape[2] == FF
    if planar:
        piece = gather_rows(normed, 1, 0).reshape(-1, width)
    else:
        piece = lax.all_gather(normed, "expert", axis=0, tiled=True)
    query_part = jnp.dot(piece, query_weight, preferred_element_type=jnp.float32).astype(
        jnp.bfloat16
    )
    key_part = jnp.dot(piece, key_weight, preferred_element_type=jnp.float32).astype(jnp.bfloat16)
    value_part = jnp.dot(piece, value_weight, preferred_element_type=jnp.float32).astype(
        jnp.bfloat16
    )
    projected = jnp.concatenate([query_part, key_part, value_part], axis=1)
    layout = (requests, SB, heads_here, HD)
    queries = projected[:, :local_width].reshape(layout)
    new_keys = projected[:, local_width : 2 * local_width].reshape(layout)
    new_values = projected[:, 2 * local_width :].reshape(layout)
    scale = HD ** (-0.5)
    positions = jnp.arange(SB, dtype=jnp.int32)
    own_scores = (
        jnp.einsum("rihd,rjhd->rhij", queries, new_keys, preferred_element_type=jnp.float32) * scale
    )
    own_scores = jnp.where(
        positions[None, None, None, :] < own_length[:, None, None, None], own_scores, -jnp.inf
    )
    member = group_index[0]
    prompt_positions = jnp.arange(longest, dtype=jnp.int32)

    def group_step(group, attended):
        first = jnp.sum((member < group).astype(jnp.int32))
        start = jnp.minimum(first, requests - GSIZE)
        window_queries = lax.dynamic_slice_in_dim(queries, start, GSIZE, 0)
        group_keys = lax.dynamic_index_in_dim(prompt_keys, group, 0, keepdims=False).reshape(
            longest, heads_here, HD
        )
        group_values = lax.dynamic_index_in_dim(prompt_values, group, 0, keepdims=False).reshape(
            longest, heads_here, HD
        )
        scores = (
            jnp.einsum(
                "rihd,jhd->rhij", window_queries, group_keys, preferred_element_type=jnp.float32
            )
            * scale
        )
        limit = lax.dynamic_index_in_dim(prompt_length, group, 0, keepdims=False)
        scores = jnp.where(prompt_positions < limit, scores, -jnp.inf)
        window_own = lax.dynamic_slice_in_dim(own_scores, start, GSIZE, 0)
        highest = jnp.maximum(jnp.max(scores, axis=-1), jnp.max(window_own, axis=-1))
        prompt_weights = jnp.exp(scores - highest[..., None]).astype(jnp.bfloat16)
        own_weights = jnp.exp(window_own - highest[..., None]).astype(jnp.bfloat16)
        window_values = lax.dynamic_slice_in_dim(new_values, start, GSIZE, 0)
        summed = jnp.einsum(
            "rhij,jhd->rihd", prompt_weights, group_values, preferred_element_type=jnp.float32
        )
        summed = summed + jnp.einsum(
            "rhij,rjhd->rihd", own_weights, window_values, preferred_element_type=jnp.float32
        )
        totals = jnp.sum(prompt_weights, axis=-1, dtype=jnp.float32) + jnp.sum(
            own_weights, axis=-1, dtype=jnp.float32
        )
        result = (summed / jnp.transpose(totals, (0, 2, 1))[..., None]).astype(jnp.bfloat16)
        inside = lax.dynamic_slice_in_dim(member, start, GSIZE, 0) == group
        current = lax.dynamic_slice_in_dim(attended, start, GSIZE, 0)
        merged = jnp.where(inside[:, None, None, None], result, current)
        return lax.dynamic_update_slice_in_dim(attended, merged, start, 0)

    attended = lax.fori_loop(0, groups_here, group_step, jnp.zeros(layout, jnp.bfloat16))
    flat_attended = attended.reshape(requests * SB, local_width)
    piece = flat_attended
    update_part = jnp.dot(piece, output_weight, preferred_element_type=jnp.float32).astype(
        jnp.bfloat16
    )
    if planar:
        attention_update = scatter_sum(update_part.reshape(1, 8, tok_rows, width), 1)
    else:
        attention_update = lax.psum_scatter(
            update_part, "expert", scatter_dimension=0, tiled=True
        )
    expert_input = rms_scale(
        residual_in.astype(jnp.float32) + attention_update.astype(jnp.float32), expert_gain
    )
    if planar:
        expert_update = experts_by_plane(
            expert_input, expert_ids, expert_mix, gate_weight, up_weight, down_weight
        )
        return (attention_update, expert_update)
    data_groups = lax.axis_size("dp")
    expert_groups = lax.axis_size("expert")
    devices = data_groups * expert_groups
    hidden_split = FF // gate_weight.shape[2]
    experts = devices // hidden_split
    capacity = max(2, tok_rows * TOP * 3 // (2 * experts))
    chosen = expert_ids.reshape(-1)
    routes_here = chosen.shape[0]
    owners = jnp.arange(routes_here, dtype=jnp.int32) // TOP
    matches = (chosen[:, None] == jnp.arange(experts, dtype=jnp.int32)[None, :]).astype(jnp.int32)
    slots = jnp.sum((jnp.cumsum(matches, axis=0) - matches) * matches, axis=1)
    table = (
        jnp.full((experts * capacity,), tok_rows, jnp.int32)
        .at[chosen * capacity + slots]
        .set(owners)
    )
    padded = jnp.concatenate([expert_input, jnp.zeros((1, width), jnp.bfloat16)], axis=0)
    outgoing = jnp.broadcast_to(
        padded[table].reshape(experts, 1, capacity, width), (experts, hidden_split, capacity, width)
    )
    outgoing = outgoing.reshape(devices, capacity, width)
    returned = lax.all_to_all(
        expert_block(
            lax.all_to_all(outgoing, ("dp", "expert"), split_axis=0, concat_axis=0, tiled=True),
            gate_weight,
            up_weight,
            down_weight,
        ),
        ("dp", "expert"),
        split_axis=0,
        concat_axis=0,
        tiled=True,
    )
    pieces = returned.reshape(experts, hidden_split, capacity, width)[chosen, :, slots]
    blended = jnp.sum(pieces.astype(jnp.float32), axis=1) * expert_mix.reshape(-1)[:, None]
    expert_update = jnp.sum(blended.reshape(tok_rows, TOP, width), axis=1).astype(jnp.bfloat16)
    return (attention_update, expert_update)


def solution(mesh):
    in_specs = (
        P(("dp", "expert"), None),
        P(),
        P(None, "expert"),
        P(None, "expert"),
        P(None, "expert"),
        P("expert", None),
        P("dp", None, "expert"),
        P("dp", None, "expert"),
        P("dp", None),
        P("dp"),
        P("dp"),
        P(),
        P(("dp", "expert"), None),
        P(("dp", "expert"), None),
        P(("dp", "expert"), None, None),
        P(("dp", "expert"), None, None),
        P(("dp", "expert"), None, None),
    )
    out_specs = (P(("dp", "expert"), None), P(("dp", "expert"), None))
    return jax.shard_map(
        per_device, mesh=mesh, in_specs=in_specs, out_specs=out_specs, check_vma=False
    )
```
